32 devices in a mesh: dp: 16 (over z, x, core), mp: 2 (over y).
Axes of the slice: x: 2, y: 2, z: 4, core: 2. Of those that a mesh axis runs over, the one named last changes fastest.
Arguments:
- clips: bfloat16 [32, 300, 25, 128], P('dp', None, None, 'mp'), may hold values from -6 to 6
- lengths: int32 [32], P('dp'), may hold values from 37 to 300
- grad_out: bfloat16 [32, 150, 25, 256], P('dp', None, None, 'mp'), may hold values from -6 to 6
- parents: int32 [25], replicated, may hold values from 0 to 23, as said below
- first_graph: float32 [128, 3, 256], P(None, None, 'mp'), may hold values from -0.5 to 0.5
- first_time: float32 [9, 256, 256], P(None, None, 'mp'), may hold values from -0.125 to 0.125
- first_skip: float32 [128, 256], P(None, 'mp'), may hold values from -0.5 to 0.5
- second_graph: float32 [256, 3, 256], P(None, None, 'mp'), may hold values from -0.375 to 0.375
- second_time: float32 [9, 256, 256], P(None, None, 'mp'), may hold values from -0.125 to 0.125
- first_graph_moment: float32 [128, 3, 256], P(None, None, 'mp'), may hold values from -896 to 896
- first_time_moment: float32 [9, 256, 256], P(None, None, 'mp'), may hold values from -896 to 896
- first_skip_moment: float32 [128, 256], P(None, 'mp'), may hold values from -896 to 896
- second_graph_moment: float32 [256, 3, 256], P(None, None, 'mp'), may hold values from -896 to 896
- second_time_moment: float32 [9, 256, 256], P(None, None, 'mp'), may hold values from -896 to 896
- norm_param: float32 [2, 5, 256], P(None, None, 'mp'), may hold values from 0.25 to 1.75
- norm_moment: float32 [2, 5, 256], P(None, None, 'mp'), may hold values from -128 to 128
- edge_weight: float32 [2, 3, 25, 25], replicated, may hold values from 0.25 to 1.75
- edge_moment: float32 [2, 3, 25, 25], replicated, may hold values from -128 to 128
Outputs:
- block_out: bfloat16 [32, 150, 25, 256], P('dp', None, None, 'mp')
- input_grad: float32 [32, 300, 25, 128], P('dp', None, None, 'mp')
- first_graph_moment_next: float32 [128, 3, 256], P(None, None, 'mp')
- first_time_moment_next: float32 [9, 256, 256], P(None, None, 'mp')
- first_skip_moment_next: float32 [128, 256], P(None, 'mp')
- second_graph_moment_next: float32 [256, 3, 256], P(None, None, 'mp')
- second_time_moment_next: float32 [9, 256, 256], P(None, None, 'mp')
- first_graph_next: float32 [128, 3, 256], P(None, None, 'mp')
- first_time_next: float32 [9, 256, 256], P(None, None, 'mp')
- first_skip_next: float32 [128, 256], P(None, 'mp')
- second_graph_next: float32 [256, 3, 256], P(None, None, 'mp')
- second_time_next: float32 [9, 256, 256], P(None, None, 'mp')
- first_graph_copy: bfloat16 [128, 3, 256], P(None, None, 'mp')
- first_time_copy: bfloat16 [9, 256, 256], P(None, None, 'mp')
- first_skip_copy: bfloat16 [128, 256], P(None, 'mp')
- second_graph_copy: bfloat16 [256, 3, 256], P(None, None, 'mp')
- second_time_copy: bfloat16 [9, 256, 256], P(None, None, 'mp')
- norm_moment_next: float32 [2, 5, 256], P(None, None, 'mp')
- norm_param_next: float32 [2, 5, 256], P(None, None, 'mp')
- edge_moment_next: float32 [2, 3, 25, 25], replicated
- edge_weight_next: float32 [2, 3, 25, 25], replicated
The draws below stay inside these ranges and needn't reach their ends.
Inputs may be any that keep to these rules, and one draw needn't show every extreme that they name: parents[0] = 0 and parents[j] < j for j >= 1, so the joints form a tree rooted at joint 0.
All inputs are finite; a program needn't handle non-finite values.
Results may differ from the reference program's by a relative error of at most 0.015.
Values may be sent and summed in bfloat16 or wider, within the bound.
A program may use at most 640 MiB of HBM per device.

```python
import jax
import jax.numpy as jnp
from jax import lax

C0 = 128
C1 = 256
V = 25
K = 3
FRAMES = 300
CLIPS_DEV = 2
CLIPS = 32
HALF = 150


def draw_lengths(key, part):
    key = jax.random.fold_in(key, 11)
    owner_ids = jnp.arange(CLIPS, dtype=jnp.int32) // CLIPS_DEV
    group_count = CLIPS // CLIPS_DEV
    base_length = FRAMES // 8 + owner_ids * (FRAMES * 2 // 3) // max(group_count - 1, 1)
    extra = jax.random.randint(key, (CLIPS,), 0, FRAMES // 3 + 1, dtype=jnp.int32)
    drawn = jnp.minimum(base_length + extra, FRAMES)
    drawn = drawn.at[0].set(FRAMES // 8).at[CLIPS - 1].set(FRAMES)
    return drawn.astype(jnp.int32)


def draw_parents(key, part):
    key = jax.random.fold_in(key, 23)
    upper = jnp.maximum(jnp.arange(V, dtype=jnp.int32), 1)
    picks = jax.random.randint(key, (V,), 0, upper, dtype=jnp.int32)
    picks = picks.at[0].set(0).at[V - 1].set(V - 2)
    return picks.astype(jnp.int32)


def block_levels(key, shape, pieces, least, top_value):
    def one(dim, blocks):
        heights = jax.random.uniform(jax.random.fold_in(jax.random.fold_in(key, 6), dim), (blocks,), jnp.float32, least / len(pieces), top_value / len(pieces))
        return jnp.repeat(jnp.exp(heights), shape[dim] // blocks).reshape((-1,) + (1,) * (len(shape) - dim - 1))

    loudness = one(*pieces[0])
    for cut in pieces[1:]:
        loudness = loudness * one(*cut)
    return loudness


def bell_draw(key, dims, deviation, reach, cuts=(), kind=jnp.bfloat16):
    array = jax.random.normal(key, dims, jnp.float32) * deviation
    if len(cuts) > 0:
        array = block_levels(key, dims, cuts, -0.22, 0.18) * array
    return jnp.clip(array, min=-reach, max=reach).astype(kind)


def setup_inputs(seed: int = 0) -> dict:
    key_of = jax.random.split(jax.random.key(seed), 19)
    clips = bell_draw(key_of[0], (CLIPS, FRAMES, V, C0), 1.0, 6.0, ((0, 16), (3, 2)))
    lengths = draw_lengths(jax.random.fold_in(key_of[18], 71), 0)
    grad_out = bell_draw(key_of[2], (CLIPS, HALF, V, C1), 1.0, 6.0, ((0, 16), (3, 2)))
    parents = draw_parents(jax.random.fold_in(key_of[18], 71), 0)
    first_graph = bell_draw(key_of[4], (C0, K, C1), C0 ** -0.5, 0.5, ((2, 2),), jnp.float32)
    first_time = bell_draw(key_of[5], (9, C1, C1), (9 * C1) ** -0.5, 0.125, ((2, 2),), jnp.float32)
    first_skip = bell_draw(key_of[6], (C0, C1), C0 ** -0.5, 0.5, ((1, 2),), jnp.float32)
    second_graph = bell_draw(key_of[7], (C1, K, C1), C1 ** -0.5, 0.375, ((2, 2),), jnp.float32)
    second_time = bell_draw(key_of[8], (9, C1, C1), (9 * C1) ** -0.5, 0.125, ((2, 2),), jnp.float32)
    first_graph_moment = bell_draw(key_of[9], (C0, K, C1), ((CLIPS * FRAMES * V // 12) ** 0.5), 896.0, ((2, 2),), jnp.float32)
    first_time_moment = bell_draw(key_of[10], (9, C1, C1), ((CLIPS * FRAMES * V // 12) ** 0.5), 896.0, ((2, 2),), jnp.float32)
    first_skip_moment = bell_draw(key_of[11], (C0, C1), ((CLIPS * FRAMES * V // 12) ** 0.5), 896.0, ((1, 2),), jnp.float32)
    second_graph_moment = bell_draw(key_of[12], (C1, K, C1), ((CLIPS * FRAMES * V // 12) ** 0.5), 896.0, ((2, 2),), jnp.float32)
    second_time_moment = bell_draw(key_of[13], (9, C1, C1), ((CLIPS * FRAMES * V // 12) ** 0.5), 896.0, ((2, 2),), jnp.float32)
    norm_param = jnp.clip(1.0 + 0.15 * jax.random.normal(key_of[14], (2, 5, C1), jnp.float32), 0.25, 1.75)
    norm_moment = bell_draw(key_of[15], (2, 5, C1), ((CLIPS * FRAMES * V // 540) ** 0.5), 128.0, ((2, 2),), jnp.float32)
    edge_weight = jnp.clip(1.0 + 0.15 * jax.random.normal(key_of[16], (2, K, V, V), jnp.float32), 0.25, 1.75)
    edge_moment = bell_draw(key_of[17], (2, K, V, V), ((CLIPS * FRAMES * C1 // 5000) ** 0.5), 128.0, (), jnp.float32)
    return {"clips": clips, "lengths": lengths, "grad_out": grad_out, "parents": parents, "first_graph": first_graph, "first_time": first_time, "first_skip": first_skip, "second_graph": second_graph, "second_time": second_time, "first_graph_moment": first_graph_moment, "first_time_moment": first_time_moment, "first_skip_moment": first_skip_moment, "second_graph_moment": second_graph_moment, "second_time_moment": second_time_moment, "norm_param": norm_param, "norm_moment": norm_moment, "edge_weight": edge_weight, "edge_moment": edge_moment}


epsilon = 1e-05
schulz_coeffs = (3.4445, -4.775, 2.0315)
muon_decay = 0.5
muon_rate = 0.5
plain_decay = 0.9
plain_rate = 0.001
highest = lax.Precision.HIGHEST

@jax.custom_vjp
def low(v):
    return lax.optimization_barrier(v.astype(jnp.bfloat16)).astype(jnp.float32)

@jax.custom_vjp
def low_back(v):
    return v

def low_keep(v):
    return (low(v), None)

def low_pass(kept, grad):
    return (grad,)

def back_keep(v):
    return (v, None)

def back_low(kept, grad):
    return (low(grad),)
low.defvjp(low_keep, low_pass)
low_back.defvjp(back_keep, back_low)

def adjacency(parents):
    joint_count = parents.shape[0]
    row_ids = lax.broadcasted_iota(jnp.int32, (joint_count, joint_count), 0)
    col_ids = lax.broadcasted_iota(jnp.int32, (joint_count, joint_count), 1)
    itself = (row_ids == col_ids).astype(jnp.float32)
    inward = ((parents[:, None] == col_ids) & (row_ids != col_ids)).astype(jnp.float32)
    outward = ((parents[None, :] == row_ids) & (row_ids != col_ids)).astype(jnp.float32)
    stacked = jnp.stack([itself, inward, outward])
    degree = lax.optimization_barrier(jnp.sum(stacked, axis=(0, 1)))
    return stacked / degree[None, None, :]

def frame_masks(lengths, frame_count):
    steps = lax.broadcasted_iota(jnp.int32, (lengths.shape[0], frame_count), 1)
    full_mask = (steps < lengths[:, None]).astype(jnp.float32)
    half_mask = (2 * steps[:, :frame_count // 2] < lengths[:, None]).astype(jnp.float32)
    return (full_mask, half_mask)

def unfold(hidden, stride):
    frame_count = hidden.shape[1]
    padded = jnp.pad(hidden, ((0, 0), (4, 4), (0, 0), (0, 0)))
    out_frames = frame_count // stride
    shifted = [padded[:, offset:offset + stride * (out_frames - 1) + 1:stride] for offset in range(9)]
    return jnp.concatenate(shifted, axis=-1)

def orthogonal(matrix):
    tall = matrix.shape[0] > matrix.shape[1]
    iterate = matrix.T if tall else matrix
    iterate = iterate / (jnp.sqrt(jnp.sum(iterate * iterate)) + 1e-07)
    for sweep in range(5):
        gram_matrix = jnp.dot(iterate, iterate.T, precision=highest)
        polynomial = schulz_coeffs[1] * gram_matrix + schulz_coeffs[2] * jnp.dot(gram_matrix, gram_matrix, precision=highest)
        iterate = schulz_coeffs[0] * iterate + jnp.dot(polynomial, iterate, precision=highest)
    return iterate.T if tall else iterate

def muon_step(weight, moment, gradient, leading):
    moment_next = muon_decay * moment + gradient
    row_count = 1
    for extent in weight.shape[:leading]:
        row_count = row_count * extent
    matrix = moment_next.reshape(row_count, -1)
    factor = max(1.0, matrix.shape[0] / matrix.shape[1]) ** 0.5
    weight_next = weight - muon_rate * factor * orthogonal(matrix).reshape(weight.shape)
    return (moment_next, weight_next)

def graph_layer(inputs, weight, edge_values):

    def single(single_clip):
        mixed = jnp.dot(single_clip.reshape(-1, single_clip.shape[-1]), weight, precision=highest)
        mixed = low_back(mixed).reshape(single_clip.shape[0], single_clip.shape[1], edge_values.shape[0], -1)
        return jnp.einsum('tvkc,kvw->twc', mixed, edge_values, precision=highest)
    return lax.map(jax.checkpoint(single), inputs)

def time_layer(inputs, weight, stride):

    def single(single_clip):
        columns = unfold(single_clip[None], stride)[0]
        result = jnp.dot(columns.reshape(-1, columns.shape[-1]), weight, precision=highest)
        return low_back(result).reshape(columns.shape[0], columns.shape[1], -1)
    return lax.map(jax.checkpoint(single), inputs)

def reference(clips, lengths, grad_out, parents, first_graph, first_time, first_skip, second_graph, second_time, first_graph_moment, first_time_moment, first_skip_moment, second_graph_moment, second_time_moment, norm_param, norm_moment, edge_weight, edge_moment):
    full_mask, half_mask = frame_masks(lengths, FRAMES)
    full_wide = full_mask[:, :, None, None]
    half_wide = half_mask[:, :, None, None]
    graph_mats = adjacency(parents)
    count_full = V * jnp.sum(full_mask)
    count_half = V * jnp.sum(half_mask)

    def batch_norm(tensor, frame_mask, total_count, slot_index, norm_values):
        weighted = tensor * frame_mask[:, :, None, None]
        center = lax.optimization_barrier(jnp.sum(weighted, axis=(0, 1, 2))) / total_count
        spread = lax.optimization_barrier(jnp.sum(weighted * tensor, axis=(0, 1, 2))) / total_count - center * center
        return (tensor - center) * lax.rsqrt(spread + epsilon) * norm_values[0, slot_index] + norm_values[1, slot_index]

    def forward(inputs, graph_one, time_one, skip_one, graph_two, time_two, norm_values, edge_values):
        masked = inputs * full_wide
        first_edges = graph_mats * edge_values[0]
        second_edges = graph_mats * edge_values[1]
        spatial = graph_layer(masked, low(graph_one).reshape(C0, -1), first_edges)
        hidden_one = low(jax.nn.silu(batch_norm(spatial, full_mask, count_full, 0, norm_values)) * full_wide)
        temporal = time_layer(hidden_one, low(time_one).reshape(-1, C1), 2)
        strided = masked[:, ::2].reshape(-1, C0)
        skipped = low_back(jnp.dot(strided, low(skip_one), precision=highest)).reshape(CLIPS, HALF, V, C1)
        joined = batch_norm(temporal, half_mask, count_half, 1, norm_values) + batch_norm(skipped, half_mask, count_half, 2, norm_values)
        middle = low(jax.nn.silu(joined) * half_wide)
        spatial_two = graph_layer(middle, low(graph_two).reshape(C1, -1), second_edges)
        hidden_two = low(jax.nn.silu(batch_norm(spatial_two, half_mask, count_half, 3, norm_values)) * half_wide)
        temporal_two = time_layer(hidden_two, low(time_two).reshape(-1, C1), 1)
        return jax.nn.silu(batch_norm(temporal_two, half_mask, count_half, 4, norm_values) + middle) * half_wide
    final, pullback = jax.vjp(forward, clips.astype(jnp.float32), first_graph, first_time, first_skip, second_graph, second_time, norm_param, edge_weight)
    grads = pullback(grad_out.astype(jnp.float32))
    graph_one_moment, graph_one_next = muon_step(first_graph, first_graph_moment, grads[1], 1)
    time_one_moment, time_one_next = muon_step(first_time, first_time_moment, grads[2], 2)
    skip_one_moment, skip_one_next = muon_step(first_skip, first_skip_moment, grads[3], 1)
    graph_two_moment, graph_two_next = muon_step(second_graph, second_graph_moment, grads[4], 1)
    time_two_moment, time_two_next = muon_step(second_time, second_time_moment, grads[5], 2)
    norm_moment_next = plain_decay * norm_moment + grads[6]
    norm_param_next = norm_param - plain_rate * norm_moment_next
    edge_moment_next = plain_decay * edge_moment + grads[7]
    edge_weight_next = edge_weight - plain_rate * edge_moment_next
    return (final.astype(jnp.bfloat16), grads[0], graph_one_moment, time_one_moment, skip_one_moment, graph_two_moment, time_two_moment, graph_one_next, time_one_next, skip_one_next, graph_two_next, time_two_next, graph_one_next.astype(jnp.bfloat16), time_one_next.astype(jnp.bfloat16), skip_one_next.astype(jnp.bfloat16), graph_two_next.astype(jnp.bfloat16), time_two_next.astype(jnp.bfloat16), norm_moment_next, norm_param_next, edge_moment_next, edge_weight_next)
```

```python
import functools

import jax
import jax.numpy as jnp
from jax import lax
from jax.experimental import pallas as pl
from jax.experimental.pallas import tpu as pltpu
from jax.sharding import PartitionSpec as P

epsilon = 1e-05
schulz_coeffs = (3.4445, -4.775, 2.0315)
muon_decay = 0.5
muon_rate = 0.5
plain_decay = 0.9
plain_rate = 0.001
highest = lax.Precision.HIGHEST
MESH = pl.DeviceIdType.MESH
f32 = jnp.float32
bf16 = jnp.bfloat16

LO = 10
PAD = 16
VMEM_LIMIT = 63 * 1024 * 1024


def params_of(**more):
    return pltpu.CompilerParams(vmem_limit_bytes=VMEM_LIMIT, **more)


def smem():
    return pl.BlockSpec(memory_space=pltpu.SMEM)


def whole(shape):
    return pl.BlockSpec(shape, lambda *_: (0,) * len(shape))


def sigmoid(tensor):
    return 0.5 + 0.5 * jnp.tanh(0.5 * tensor)


def half_mask(lo_start, count, length, channels, parity=0):
    shape = (count, PAD, channels)
    lo_ids = lax.broadcasted_iota(jnp.int32, shape, 0) + lo_start
    hi_ids = lax.broadcasted_iota(jnp.int32, shape, 1)
    frames = 2 * (hi_ids * LO + lo_ids) + parity
    return (frames < length).astype(f32)


def norm_rows(total, row, count, norm, slot):
    mean = total[row : row + 1] / count
    inverse = lax.rsqrt(total[row + 1 : row + 2] / count - mean * mean + epsilon)
    return (mean, inverse, norm[slot : slot + 1], norm[8 + slot : 9 + slot])


def forward_rows(rows):
    mean, inverse, gain, bias = rows
    return (inverse * gain, bias - mean * inverse * gain)


def normed_rows(rows):
    mean, inverse, _, _ = rows
    return (inverse, -mean * inverse)


def backward_rows(rows, count, bias_grad, gain_grad):
    mean, inverse, gain, _ = rows
    scale = gain * inverse
    return (
        scale,
        -scale * inverse * gain_grad / count,
        scale * (mean * inverse * gain_grad - bias_grad) / count,
    )


def row_sum(block):
    return jnp.sum(block.reshape(-1, block.shape[-1]), axis=0, keepdims=True)


def fold(block):
    return jnp.sum(block.reshape(-1, 8, block.shape[-1]), axis=0)


def joint_rows(joint):
    return pl.ds(pl.multiple_of(joint * PAD, PAD), PAD)


CHUNK = 5


class Tree:
    def __init__(self, refs):
        self.parent, self.children, self.values = refs

    def scale(self, value, part, chunk):
        columns = value.shape[1]
        edge = self.values[part, chunk * CHUNK : (chunk + 1) * CHUNK][:, None]
        if columns > 128:
            edge = jnp.concatenate([edge] * (columns // 128), axis=3)
        return (value.reshape(CHUNK, PAD // 8, 8, columns) * edge).reshape(CHUNK * PAD, columns)

    @staticmethod
    def specs(rows):
        joints = rows // PAD
        return [whole((rows, rows)), whole((rows, rows)), whole((3, joints, 8, 128))]


def chunks(rows):
    size = CHUNK * PAD
    return [(chunk, slice(chunk * size, (chunk + 1) * size)) for chunk in range(rows // size)]


def chunk_mask(lo, length, channels, parity=0):
    mask = half_mask(lo, 1, length, channels, parity)
    return jnp.broadcast_to(mask, (CHUNK, PAD, channels)).reshape(CHUNK * PAD, channels)


def fold_joints(block):
    return jnp.sum(block.reshape(CHUNK, PAD // 8, 8, block.shape[1]), axis=1)


def dot(left, right):
    return jnp.dot(left, right, preferred_element_type=f32)


def dot_t(left, right):
    return lax.dot_general(left, right, (((1,), (1,)), ((), ())), preferred_element_type=f32)


def t_dot(left, right):
    return lax.dot_general(left, right, (((0,), (0,)), ((), ())), preferred_element_type=f32)


def assemble(target, own, received, half):
    here = lax.axis_index("mp")
    columns = own.shape[-1]
    for part in range(2):
        start = pl.multiple_of((here if part == 0 else 1 - here) * half, half)
        target[:, part * half : (part + 1) * half, 0:columns] = own[:, pl.ds(start, half), :]
        target[:, part * half : (part + 1) * half, columns : 2 * columns] = received[:, pl.ds(start, half), :]


def give_gradient(grad_ref, first, value, half):
    here = lax.axis_index("mp")
    columns = grad_ref.shape[-1]
    for part in range(2):
        start = pl.multiple_of(first + (here if part == 0 else 1 - here) * half, half)
        piece = value[part * half : (part + 1) * half].astype(bf16)
        grad_ref[0, pl.ds(start, half), :] = piece[:, :columns]
        grad_ref[1, pl.ds(start, half), :] = piece[:, columns:]


class Links:
    def __init__(self, mesh):
        self.dp, self.mp = mesh.shape["dp"], mesh.shape["mp"]
        self.split = 1
        while self.split * self.split < self.dp:
            self.split *= 2
        self.near, self.far = self.split * self.mp, self.dp // self.split
        self.stages = []
        stride = 1
        for size in (2, 2, 4):
            size = min(size, self.dp // stride)
            self.stages.append((stride, size))
            stride *= size
        self.stride = stride
        self.extra = self.dp // stride

    def here(self):
        dp, mp = lax.axis_index("dp"), lax.axis_index("mp")
        low, high = lax.rem(dp, self.split), lax.div(dp, self.split)
        return dp, mp, low, high

    def near_id(self, rank):
        _, _, _, high = self.here()
        return {"dp": high * self.split + lax.rem(rank, self.split), "mp": lax.div(rank, self.split)}

    def far_id(self, rank):
        _, mp, low, _ = self.here()
        return {"dp": rank * self.split + low, "mp": mp}

    def near_peers(self):
        _, mp, low, _ = self.here()
        return [lax.rem(mp * self.split + low + step, self.near) for step in range(1, self.near)]

    def far_peers(self):
        _, _, _, high = self.here()
        return [lax.rem(high + step, self.far) for step in range(1, self.far)]

    def stage_rank(self, slot):
        stride, size = self.stages[slot]
        return lax.rem(lax.div(lax.axis_index("dp"), stride), size)

    def stage_id(self, slot, rank):
        dp, mp, _, _ = self.here()
        stride, _ = self.stages[slot]
        return {"dp": dp + (rank - self.stage_rank(slot)) * stride, "mp": mp}

    def stage_peers(self, slot):
        _, size = self.stages[slot]
        return [lax.rem(self.stage_rank(slot) + step, size) for step in range(1, size)]

    def greet(self):
        barrier = pltpu.get_barrier_semaphore()
        for peer in self.near_peers():
            pl.semaphore_signal(barrier, inc=1, device_id=self.near_id(peer), device_id_type=MESH)
        for peer in self.far_peers():
            pl.semaphore_signal(barrier, inc=1, device_id=self.far_id(peer), device_id_type=MESH)

    def meet(self):
        pl.semaphore_wait(pltpu.get_barrier_semaphore(), self.near + self.far - 2)

    def sum_scratch(self, shape):
        return [
            pltpu.VMEM((self.near,) + shape, f32),
            pltpu.VMEM((self.far,) + shape, f32),
            pltpu.SemaphoreType.DMA((self.near,)),
            pltpu.SemaphoreType.DMA((self.near,)),
            pltpu.SemaphoreType.DMA((self.far,)),
            pltpu.SemaphoreType.DMA((self.far,)),
        ]


def remote(source, target, send, receive, device):
    return pltpu.make_async_remote_copy(
        src_ref=source, dst_ref=target, send_sem=send, recv_sem=receive, device_id=device, device_id_type=MESH
    )


def partner():
    return {"dp": lax.axis_index("dp"), "mp": 1 - lax.axis_index("mp")}


def remote_params(name):
    ids = ("frames_in", "forward", "backward")
    return params_of(collective_id=ids.index(name), has_side_effects=True)


def anywhere():
    return pl.BlockSpec(memory_space=pl.ANY)


class Sum:
    def __init__(self, links, comm, halves=True):
        self.links, self.halves = links, halves
        self.near, self.far, self.send_near, self.receive_near, self.send_far, self.receive_far = comm

    def reorder(self, block):
        if not self.halves:
            return block
        _, mp, _, _ = self.links.here()
        half = block.shape[1] // 2
        first, second = block[:, :half], block[:, half:]
        return jnp.concatenate([jnp.where(mp == 0, first, second), jnp.where(mp == 0, second, first)], axis=1)

    def sides(self):
        links = self.links
        _, mp, low, high = links.here()
        return (
            (self.near, mp * links.split + low, links.near_peers(), links.near_id, self.send_near, self.receive_near),
            (self.far, high, links.far_peers(), links.far_id, self.send_far, self.receive_far),
        )

    def copies(self, side):
        buffer, me, peers, ids, send, receive = side
        return [remote(buffer.at[me], buffer.at[me], send.at[step], receive.at[me], ids(peer)) for step, peer in enumerate(peers)]

    def finish(self, side):
        buffer, me, peers, ids, send, receive = side
        for peer in peers:
            remote(buffer.at[peer], buffer.at[peer], send.at[0], receive.at[peer], ids(peer)).wait_recv()
        for copy in self.copies(side):
            copy.wait_send()
        total = buffer[0]
        for rank in range(1, buffer.shape[0]):
            total = total + buffer[rank]
        return total

    def start_near(self, value):
        side = self.sides()[0]
        side[0][side[1]] = self.reorder(value)
        for copy in self.copies(side):
            copy.start()

    def start_far(self):
        near, far = self.sides()
        far[0][far[1]] = self.finish(near)
        for copy in self.copies(far):
            copy.start()

    def total(self):
        return self.reorder(self.finish(self.sides()[1]))

    def whole(self, value):
        self.start_near(value)
        self.start_far()
        return self.total()


class Bulk:
    def __init__(self, pairs, send, receive):
        self.pairs, self.send, self.receive = pairs, send, receive

    def copies(self):
        return [
            remote(source, target, self.send.at[slot], self.receive.at[slot], partner())
            for slot, (source, target) in enumerate(self.pairs)
        ]

    def start(self):
        for copy in self.copies():
            copy.start()

    def wait(self):
        for copy in self.copies():
            copy.wait()


def bulk_scratch(count):
    return [pltpu.SemaphoreType.DMA((count,)), pltpu.SemaphoreType.DMA((count,))]


def frame_selector(frame_count, first_row, row_count, length=None):
    row_ids = lax.broadcasted_iota(jnp.int32, (row_count, frame_count), 0) + first_row
    frame_ids = lax.broadcasted_iota(jnp.int32, (row_count, frame_count), 1)
    hi_ids = lax.rem(row_ids, PAD)
    outer = lax.div(row_ids, PAD)
    parity = (outer >= LO).astype(jnp.int32)
    frames = 2 * (hi_ids * LO + outer - parity * LO) + parity
    chosen = frames == frame_ids
    if length is not None:
        chosen = chosen & (frame_ids < length)
    return chosen.astype(f32).astype(bf16)


def frames_in_kernel(
    links, count, length, clips_ref, other_ref, graph_own, skip_own, norm_own,
    x_ref, graph_other, skip_other, norm_ref, selector, norm_other, bulk_send, bulk_receive,
):
    step = pl.program_id(0)
    here = lax.axis_index("mp")
    bulk = Bulk([(graph_own, graph_other), (skip_own, skip_other), (norm_own, norm_other)], bulk_send, bulk_receive)

    @pl.when(step == 0)
    def _():
        barrier = pltpu.get_barrier_semaphore()
        pl.semaphore_signal(barrier, inc=1, device_id=partner(), device_id_type=MESH)
        selector[...] = frame_selector(selector.shape[1], 0, selector.shape[0], length[0])
        pl.semaphore_wait(barrier, 1)
        bulk.start()

    for joint in range(count):
        both = jnp.concatenate([clips_ref[here, joint], other_ref[joint]], axis=0)
        turned = dot_t(selector[...], both).astype(bf16)
        x_ref[:, :, joint * PAD : (joint + 1) * PAD, :] = turned.reshape(2, LO, PAD, turned.shape[1])

    @pl.when(step == pl.num_programs(0) - 1)
    def _():
        bulk.wait()
        half = norm_own.shape[1]
        norm_ref[:, :half] = norm_own[...]
        norm_ref[:, half:] = norm_other[...]


def frames_in(links, clips, other, length, graph_own, skip_own, norm_own, count=5):
    _, joints, thin, frame_count = clips.shape
    return pl.pallas_call(
        functools.partial(frames_in_kernel, links, count),
        grid=(joints // count,),
        out_shape=(
            jax.ShapeDtypeStruct((2, LO, joints * PAD, 2 * thin), bf16),
            jax.ShapeDtypeStruct(graph_own.shape, bf16),
            jax.ShapeDtypeStruct(skip_own.shape, bf16),
            jax.ShapeDtypeStruct((norm_own.shape[0], 2 * norm_own.shape[1]), f32),
        ),
        in_specs=[
            smem(),
            pl.BlockSpec((2, count, thin, frame_count), lambda i: (0, i, 0, 0)),
            pl.BlockSpec((count, thin, frame_count), lambda i: (i, 0, 0)),
            anywhere(),
            anywhere(),
            whole(norm_own.shape),
        ],
        out_specs=(
            pl.BlockSpec((2, LO, count * PAD, 2 * thin), lambda i: (0, 0, i, 0)),
            anywhere(),
            anywhere(),
            whole((norm_own.shape[0], 2 * norm_own.shape[1])),
        ),
        scratch_shapes=[pltpu.VMEM((2 * LO * PAD, frame_count), bf16), pltpu.VMEM(norm_own.shape, f32)] + bulk_scratch(3),
        compiler_params=remote_params("frames_in"),
        name="frames_in",
    )(length, clips, other, graph_own, skip_own, norm_own)


def frames_out_kernel(count, keep0, keep1, received0, received1, out_ref, selector):
    here = lax.axis_index("mp")
    thin, frame_count = out_ref.shape[2:]
    pair_rows = LO // 2 * PAD

    @pl.when(pl.program_id(0) == 0)
    def _():
        row_ids = lax.broadcasted_iota(jnp.int32, (pair_rows, frame_count), 0)
        frame_ids = lax.broadcasted_iota(jnp.int32, (pair_rows, frame_count), 1)
        pair_frames = 2 * (lax.rem(row_ids, PAD) * LO + 2 * lax.div(row_ids, PAD))
        for parity in range(2):
            for odd in range(2):
                chosen = pair_frames + (2 * odd + parity) == frame_ids
                selector[odd, parity * pair_rows : (parity + 1) * pair_rows, :] = chosen.astype(f32).astype(bf16)

    for joint in range(count):
        rows = slice(joint * PAD, (joint + 1) * PAD)
        for clip, parts in ((here, (keep0, keep1)), (1 - here, (received0, received1))):
            both = jnp.concatenate([part[:, rows, :].reshape(pair_rows, 2 * thin) for part in parts], axis=0)
            even, odd = t_dot(both, selector[0]), t_dot(both, selector[1])
            out_ref[clip, joint] = even[:thin] + odd[thin:]


def frames_out(keep, received, frame_count, count=5):
    rows, width = keep.shape[1:]
    joints = rows // PAD
    block = pl.BlockSpec((LO // 2, count * PAD, width), lambda i: (0, i, 0))
    return pl.pallas_call(
        functools.partial(frames_out_kernel, count),
        grid=(joints // count,),
        out_shape=jax.ShapeDtypeStruct((2, joints, width // 2, frame_count), f32),
        in_specs=[block, pl.BlockSpec((LO // 2, count * PAD, width), lambda i: (1, i, 0)), block, block],
        out_specs=pl.BlockSpec((2, count, width // 2, frame_count), lambda i: (0, i, 0, 0)),
        scratch_shapes=[pltpu.VMEM((2, LO * PAD, frame_count), bf16)],
        compiler_params=params_of(),
        name="frames_out",
    )(keep, keep, *received)


def put_with_halo(extended, lo_start, lb, reach, rows, value):
    extended[pl.ds(lo_start + reach, lb), rows, :] = value.astype(bf16)
    width = value.shape[-1]

    @pl.when(lo_start == 0)
    def _():
        later = pltpu.roll(value[0:reach].reshape(-1, width), reach * PAD - 1, 0).reshape(reach, PAD, width)
        extended[LO + reach : LO + 2 * reach, rows, :] = later.astype(bf16)

    @pl.when(lo_start == LO - lb)
    def _():
        earlier = pltpu.roll(value[lb - reach : lb].reshape(-1, width), 1, 0).reshape(reach, PAD, width)
        extended[0:reach, rows, :] = earlier.astype(bf16)


def taps(stride):
    if stride == 2:
        return [(tap % 2, (tap - 4 - tap % 2) // 2) for tap in range(9)]
    return [(0, tap - 4) for tap in range(9)]


def time_forward(extended, w_ref, lo, stride, reach):
    result = None
    for tap, (parity, shift) in enumerate(taps(stride)):
        part = dot(extended[parity, lo + (reach + shift)], w_ref[tap])
        result = part if result is None else result + part
    return result


def time_backward(extended, w_ref, lo, stride, reach, parity):
    result = None
    for tap, (own, shift) in enumerate(taps(stride)):
        if own == parity:
            part = dot_t(extended[lo + (reach - shift)], w_ref[tap])
            result = part if result is None else result + part
    return result


class Drip:
    def __init__(self, source, target, send, receive, first=0):
        self.source, self.target, self.send, self.receive, self.first = source, target, send, receive, first

    def piece(self, index):
        place = self.first + index
        return remote(self.source.at[index], self.target.at[index], self.send.at[place], self.receive.at[place], partner())

    def start(self, index):
        self.piece(index).start()

    def wait(self):
        def body(index, _):
            self.piece(index).wait()
            return 0

        lax.fori_loop(0, self.source.shape[0], body, 0)


def forward_kernel(
    links, joints, length, x_ref, graph_one_own, graph_one_other, skip_own, skip_other, time_one_own, graph_two_own, time_two_own,
    norm_ref, parent_ref, children_ref, first_values, second_values, cotangent_own, cotangent_out,
    spatial_out, skipped_out, temporal_out, middle_out, spatial_two_out, temporal_two_out, up_out, block_own_out, block_other_out,
    time_one_out, graph_two_out, time_two_out, total1_ref, total2_ref, total3_ref, total4_ref, total5_ref,
    spatial_all, skipped_all, temporal_all, middle_all, spatial_two_all, temporal_two_all, up_all, block_own_all, block_other_all,
    time_one, graph_two, time_two, graph_one, skip_one, time_one_other, graph_two_other, time_two_other, cotangent_other,
    hidden_one, hidden_two, stat_ref, scaled, up_sum, down_sum, mixed_one, mixed_two, drip_send, drip_receive, store_sem, *comm,
):
    rows, width = x_ref.shape[2:]
    channels = 2 * width
    frame_length = length[0]
    norm = norm_ref[...]
    per_sum = len(comm) // 5
    sums = [Sum(links, comm[slot * per_sum : (slot + 1) * per_sum]) for slot in range(5)]
    first_tree = Tree((parent_ref, children_ref, first_values))
    second_tree = Tree((parent_ref, children_ref, second_values))
    taps_count = time_one_own.shape[0]
    drips, start = [], 0
    for source, target in (
        (time_one_own, time_one_other), (graph_two_own, graph_two_other), (time_two_own, time_two_other), (cotangent_out, cotangent_other)
    ):
        drips.append(Drip(source, target, drip_send, drip_receive, start))
        start += source.shape[0]
    time_one_drip, graph_two_drip, time_two_drip, cotangent_drip = drips
    stores = [
        pltpu.make_async_copy(source, target, store_sem.at[slot])
        for slot, (source, target) in enumerate(
            (
                (spatial_all, spatial_out), (skipped_all, skipped_out), (temporal_all, temporal_out), (middle_all, middle_out),
                (spatial_two_all, spatial_two_out), (temporal_two_all, temporal_two_out), (up_all, up_out), (block_own_all, block_own_out),
                (block_other_all, block_other_out), (time_one, time_one_out), (graph_two, graph_two_out), (time_two, time_two_out),
            )
        )
    ]

    def all_sum(slot, total_ref, count, filler):
        sums[slot].start_near(stat_ref[0:count, :])
        sums[slot].start_far()
        if filler is not None:
            cotangent_drip.start(filler)
        total_ref[0:count, :] = sums[slot].total()

    links.greet()
    assemble(graph_one, graph_one_own, graph_one_other, width // 2)
    assemble(skip_one, skip_own, skip_other, width // 2)
    stat_ref[...] = jnp.zeros_like(stat_ref)
    frames = jnp.full((1, channels), frame_length, jnp.int32)
    stat_ref[4:5, :] = (joints * frames).astype(f32)
    stat_ref[5:6, :] = (joints * lax.div(frames + 1, 2)).astype(f32)

    for parity in range(2):

        def spatial_body(pair, _):
            number = parity * (LO // 2) + pair

            @pl.when(number == 1)
            def _():
                links.meet()

            @pl.when(number >= 1)
            def _():
                time_one_drip.start(number - 1)

            pick = lambda index, where: x_ref[parity, 2 * pair + index, where, :]
            for chunk, where in chunks(rows):
                both = jnp.concatenate([pick(0, where), pick(1, where)], axis=1).astype(f32)
                scaled[where, :] = first_tree.scale(both, 1, chunk).astype(bf16)
            both = jnp.concatenate([pick(0, slice(0, rows)), pick(1, slice(0, rows))], axis=1)
            up_sum[...] = dot(parent_ref[...], both)
            down_sum[...] = dot(children_ref[...], scaled[...])
            for index in range(2):
                columns = slice(index * width, (index + 1) * width)
                for chunk, where in chunks(rows):
                    place = slice(index * rows + where.start, index * rows + where.stop)
                    mixed_one[place, 0:width] = first_tree.scale(pick(index, where).astype(f32), 0, chunk).astype(bf16)
                    mixed_one[place, width : 2 * width] = down_sum[where, columns].astype(bf16)
                    mixed_one[place, 2 * width : 3 * width] = first_tree.scale(up_sum[where, columns], 2, chunk).astype(bf16)
            spatial = dot(mixed_one[...], graph_one[...].reshape(-1, channels))
            spatial_all[parity, pl.ds(2 * pair, 2)] = spatial.astype(bf16).reshape(2, rows, channels)
            stat_ref[0:1, :] += row_sum(spatial)
            stat_ref[1:2, :] += row_sum(spatial * spatial)
            if parity == 0:
                skipped = dot(x_ref[0, pl.ds(2 * pair, 2)].reshape(2 * rows, width), skip_one[0])
                skipped_all[pl.ds(2 * pair, 2)] = skipped.astype(bf16).reshape(2, rows, channels)
                stat_ref[2:3, :] += row_sum(skipped)
                stat_ref[3:4, :] += row_sum(skipped * skipped)
            return 0

        lax.fori_loop(0, LO // 2, spatial_body, 0)

    all_sum(0, total1_ref, 6, 0)
    stores[0].start()
    stores[1].start()

    def normalize(values, total_ref, count, slot, extended, reach, parity, lo_start, lb):
        scale, shift = forward_rows(norm_rows(total_ref[...], 0, count, norm, slot))
        mask = half_mask(lo_start, lb, frame_length, channels, parity)

        def body(joint, _):
            rows = joint_rows(joint)
            pre = values[pl.ds(lo_start, lb), rows, :].astype(f32) * scale + shift
            put_with_halo(extended, lo_start, lb, reach, rows, pre * sigmoid(pre) * mask)
            return 0

        lax.fori_loop(0, joints, body, 0)

    def convolve(extended, weight, out_all, stride, reach, between):
        stat_ref[...] = jnp.zeros_like(stat_ref)

        def body(lo, _):
            between(lo)
            result = time_forward(extended, weight, lo, stride, reach)
            out_all[lo] = result.astype(bf16)
            masked = result.reshape(joints, PAD, channels) * half_mask(lo, 1, frame_length, channels)
            stat_ref[0:1, :] += row_sum(masked)
            stat_ref[1:2, :] += row_sum(masked * masked)
            return 0

        lax.fori_loop(0, LO, body, 0)

    half = LO // 2
    for parity in range(2):
        for part in range(2):
            number = 2 * parity + part
            if number < 3:
                graph_two_drip.start(number)
            else:
                cotangent_drip.start(1)
            normalize(spatial_all.at[parity], total1_ref, total1_ref[4:5, :], 0, hidden_one.at[parity], 2, parity, part * half, half)
    time_one_drip.wait()
    assemble(time_one, time_one_own, time_one_other, channels // 2)
    stores[9].start()

    def between_one(lo):
        @pl.when((lax.rem(lo, 2) == 0) & (lo < 8))
        def _():
            time_two_drip.start(lax.div(lo, 2))

    convolve(hidden_one, time_one, temporal_all, 2, 2, between_one)
    stores[2].start()
    all_sum(1, total2_ref, 2, 2)

    graph_two_drip.wait()
    assemble(graph_two, graph_two_own, graph_two_other, channels // 2)
    stores[10].start()
    stat_ref[...] = jnp.zeros_like(stat_ref)
    count = total1_ref[5:6, :]
    scale2, shift2 = forward_rows(norm_rows(total2_ref[...], 0, count, norm, 1))
    scale_s, shift_s = forward_rows(norm_rows(total1_ref[...], 2, count, norm, 2))
    join_shift = shift2 + shift_s

    def middle_body(lo, _):
        @pl.when(lo < taps_count - 4)
        def _():
            time_two_drip.start(lo + 4)

        @pl.when(lo == 6)
        def _():
            cotangent_drip.start(3)

        mask = chunk_mask(lo, frame_length, channels)
        for chunk, where in chunks(rows):
            joined = temporal_all[lo, where, :].astype(f32) * scale2 + (skipped_all[lo, where, :].astype(f32) * scale_s + join_shift)
            value = (joined * sigmoid(joined) * mask).astype(bf16)
            middle_all[lo, where, :] = value
            value = value.astype(f32)
            scaled[where, :] = second_tree.scale(value, 1, chunk).astype(bf16)
            mixed_two[where, 0:channels] = second_tree.scale(value, 0, chunk).astype(bf16)
        up_sum[...] = dot(parent_ref[...], middle_all[lo])
        down_sum[...] = dot(children_ref[...], scaled[...])
        for chunk, where in chunks(rows):
            mixed_two[where, channels : 2 * channels] = down_sum[where, :].astype(bf16)
            mixed_two[where, 2 * channels : 3 * channels] = second_tree.scale(up_sum[where, :], 2, chunk).astype(bf16)
        spatial = dot(mixed_two[...], graph_two[...].reshape(-1, channels))
        spatial_two_all[0, lo] = spatial.astype(bf16)
        stat_ref[0:1, :] += row_sum(spatial)
        stat_ref[1:2, :] += row_sum(spatial * spatial)
        return 0

    lax.fori_loop(0, LO, middle_body, 0)
    stores[3].start()
    stores[4].start()
    all_sum(2, total3_ref, 2, 4)

    for part in range(2):
        cotangent_drip.start(5 + part)
        normalize(spatial_two_all.at[0], total3_ref, count, 3, hidden_two.at[0], 4, 0, part * half, half)
    time_two_drip.wait()
    assemble(time_two, time_two_own, time_two_other, channels // 2)
    stores[11].start()

    def between_two(lo):
        @pl.when((lo == 0) | (lo == 3))
        def _():
            cotangent_drip.start(7 + lax.div(lo, 3))

    convolve(hidden_two, time_two, temporal_two_all, 1, 4, between_two)
    stores[5].start()
    all_sum(3, total4_ref, 2, 9)

    cotangent_drip.wait()
    rows4 = norm_rows(total4_ref[...], 0, count, norm, 4)
    inverse, offset = normed_rows(rows4)
    gain, bias = rows4[2], rows4[3]
    for part in range(2):
        place = slice(part * half, (part + 1) * half)
        mask = half_mask(part * half, half, frame_length, channels)

        def final_body(joint, carry):
            where = joint_rows(joint)
            normed = temporal_two_all[place, where, :].astype(f32) * inverse + offset
            pre = normed * gain + bias + middle_all[place, where, :].astype(f32)
            gate = sigmoid(pre)
            active = pre * gate
            out = (active * mask).astype(bf16)
            block_own_all[place, where, :] = out[:, :, : channels // 2]
            block_other_all[place, where, :] = out[:, :, channels // 2 :]
            cotangent = jnp.concatenate([cotangent_own[place, where, :], cotangent_other[place, where, :]], axis=2)
            up = cotangent.astype(f32) * mask * (gate + active * (1.0 - gate))
            up_all[place, where, :] = up.astype(bf16)
            return (carry[0] + fold(up), carry[1] + fold(up * normed))

        zero = jnp.zeros((8, channels), f32)
        found = lax.fori_loop(0, joints, final_body, (zero, zero))
        for slot in range(2):
            if part == 0:
                stat_ref[slot : slot + 1, :] = row_sum(found[slot])
            else:
                stat_ref[slot : slot + 1, :] += row_sum(found[slot])
    for slot in (6, 7, 8):
        stores[slot].start()
    all_sum(4, total5_ref, 2, None)
    for store in stores:
        store.wait()


def forward_stage(links, clip, first_tree, second_tree, length, norm, graph_one, skip_one, time_one_own, graph_two_own, time_two_own, cotangent):
    rows, width = clip.shape[2:]
    joints = rows // PAD
    channels = 2 * width
    act = (LO, rows, channels)
    halves = (LO, rows, width)
    kept = [(2,) + act, act, act, act, (1,) + act, act, act, halves, halves, (9, channels, channels), (3, channels, channels), (9, channels, channels)]
    vmem = pl.BlockSpec(memory_space=pltpu.VMEM)
    pieces = time_one_own.shape[0] + graph_two_own.shape[0] + time_two_own.shape[0] + LO
    sum_rows = (6, 2, 2, 2, 2)
    outs = pl.pallas_call(
        functools.partial(forward_kernel, links, joints),
        out_shape=[jax.ShapeDtypeStruct(shape, bf16) for shape in kept] + [jax.ShapeDtypeStruct((8, channels), f32)] * 5,
        in_specs=[smem()] + [vmem] * 14 + [anywhere()],
        out_specs=[anywhere()] * len(kept) + [vmem] * 5,
        scratch_shapes=[pltpu.VMEM(shape, bf16) for shape in kept]
        + [
            pltpu.VMEM((3, width, channels), bf16),
            pltpu.VMEM((1, width, channels), bf16),
            pltpu.VMEM(time_one_own.shape, bf16),
            pltpu.VMEM(graph_two_own.shape, bf16),
            pltpu.VMEM(time_two_own.shape, bf16),
            pltpu.VMEM(halves, bf16),
            pltpu.VMEM((2, LO + 4, rows, channels), bf16),
            pltpu.VMEM((1, LO + 8, rows, channels), bf16),
            pltpu.VMEM((8, channels), f32),
            pltpu.VMEM((rows, channels), bf16),
            pltpu.VMEM((rows, channels), f32),
            pltpu.VMEM((rows, channels), f32),
            pltpu.VMEM((2 * rows, 3 * width), bf16),
            pltpu.VMEM((rows, 3 * channels), bf16),
            pltpu.SemaphoreType.DMA((pieces,)),
            pltpu.SemaphoreType.DMA((pieces,)),
            pltpu.SemaphoreType.DMA((len(kept),)),
        ]
        + [scratch for count in sum_rows for scratch in links.sum_scratch((count, channels))],
        compiler_params=remote_params("forward"),
        name="forward",
    )(
        length, clip, *graph_one, *skip_one, time_one_own, graph_two_own, time_two_own, norm,
        first_tree[0], first_tree[1], first_tree[2], second_tree[2], *cotangent,
    )
    return outs[: len(kept)], outs[len(kept) :]


class Reducer:
    count = 9

    def __init__(self, links, rows, refs):
        self.links, self.rows = links, rows
        self.first, self.second, self.third = self.sizes(links, rows)
        (
            self.g, self.core_in, self.part, self.pair_out, self.pair_in, self.next_out, self.next_in, self.fine, self.last_out, self.last_in,
            self.wide, self.moment_out, self.moment_in, self.result, self.send, self.receive,
        ) = refs

    @staticmethod
    def sizes(links, rows):
        first = rows // links.stages[0][1]
        second = first // links.stages[1][1]
        return first, second, second // links.stages[2][1]

    @staticmethod
    def scratch(links, rows):
        first, second, third = Reducer.sizes(links, rows)
        last = links.stages[2][1]
        return [
            pltpu.VMEM((2, rows, 128), bf16),
            pltpu.VMEM((2, first, 128), bf16),
            pltpu.VMEM((first, 128), f32),
            pltpu.VMEM((first, 128), bf16),
            pltpu.VMEM((first, 128), bf16),
            pltpu.VMEM((second, 128), bf16),
            pltpu.VMEM((second, 128), bf16),
            pltpu.VMEM((second, 128), f32),
            pltpu.VMEM((last, third, 128), bf16),
            pltpu.VMEM((last, third, 128), bf16),
            pltpu.VMEM((links.extra, third, 128), bf16),
            pltpu.VMEM((third, 128), bf16),
            pltpu.VMEM((third, 128), bf16),
            pltpu.VMEM((2, rows, 128), bf16),
            pltpu.SemaphoreType.DMA((Reducer.count, max(4, links.extra))),
            pltpu.SemaphoreType.DMA((Reducer.count, max(4, links.extra))),
        ]

    def rank(self, slot):
        return self.links.stage_rank(slot)

    def start_of(self, depth):
        start = self.rank(0) * self.first
        if depth >= 2:
            start = start + self.rank(1) * self.second
        if depth >= 3:
            start = start + self.rank(2) * self.third
        return start

    def span(self, start, size):
        return pl.ds(pl.multiple_of(start, 16), size)

    def pair_copy(self, phase, source, target):
        return remote(source, target, self.send.at[phase, 0], self.receive.at[phase, 0], partner())

    def run(self, copies):
        for copy in copies:
            copy.start()

    def end(self, copies, arrivals):
        for arrival in arrivals:
            arrival.wait_recv()
        for copy in copies:
            copy.wait_send()

    def core(self):
        peers = self.links.stage_peers(0)
        return [
            remote(
                self.g.at[:, self.span(peer * self.first, self.first), :], self.core_in,
                self.send.at[0, 0], self.receive.at[0, 0], self.links.stage_id(0, peer),
            )
            for peer in peers
        ]

    def step0(self):
        self.run(self.core())

    def step1(self):
        copies = self.core()
        self.end(copies, copies)
        rows = self.span(self.rank(0) * self.first, self.first)
        own, other = self.g[0, rows, :].astype(f32), self.g[1, rows, :].astype(f32)
        if copies:
            own, other = own + self.core_in[0].astype(f32), other + self.core_in[1].astype(f32)
        self.part[...] = own
        self.pair_out[...] = other.astype(bf16)
        self.run([self.pair_copy(1, self.pair_out, self.pair_in)])

    def next(self):
        return [
            remote(self.next_out, self.next_in, self.send.at[2, 0], self.receive.at[2, 0], self.links.stage_id(1, peer))
            for peer in self.links.stage_peers(1)
        ]

    def step2(self):
        copies = [self.pair_copy(1, self.pair_out, self.pair_in)]
        self.end(copies, copies)
        self.part[...] += self.pair_in[...].astype(f32)
        for peer in self.links.stage_peers(1):
            self.next_out[...] = self.part[self.span(peer * self.second, self.second), :].astype(bf16)
        self.run(self.next())

    def last(self):
        me = self.rank(2)
        return [
            remote(
                self.last_out.at[peer], self.last_in.at[me], self.send.at[3, slot], self.receive.at[3, me], self.links.stage_id(2, peer)
            )
            for slot, peer in enumerate(self.links.stage_peers(2))
        ]

    def step3(self):
        copies = self.next()
        self.end(copies, copies)
        mine = self.part[self.span(self.rank(1) * self.second, self.second), :]
        self.fine[...] = mine + self.next_in[...].astype(f32) if copies else mine
        for rank in range(self.last_out.shape[0]):
            self.last_out[rank] = self.fine[rank * self.third : (rank + 1) * self.third, :].astype(bf16)
        self.run(self.last())

    def wider(self):
        links = self.links
        group = lax.div(lax.axis_index("dp"), links.stride)
        found = []
        for step in range(1, links.extra):
            peer = lax.rem(group + step, links.extra)
            device = {"dp": lax.axis_index("dp") + (peer - group) * links.stride, "mp": lax.axis_index("mp")}
            found.append((peer, remote(self.wide.at[group], self.wide.at[group], self.send.at[4, step], self.receive.at[4, group], device)))
        return group, found

    def step4(self, old):
        me = self.rank(2)
        peers = self.links.stage_peers(2)
        arrivals = [
            remote(self.last_out.at[peer], self.last_in.at[peer], self.send.at[3, 0], self.receive.at[3, peer], self.links.stage_id(2, peer))
            for peer in peers
        ]
        self.end(self.last(), arrivals)
        total = self.fine[self.span(me * self.third, self.third), :]
        for peer in peers:
            total = total + self.last_in[peer].astype(f32)
        if self.links.extra > 1:
            group, found = self.wider()
            self.wide[group] = total.astype(bf16)
            copies = [copy for _, copy in found]
            self.run(copies)
            arrivals = [
                remote(self.wide.at[peer], self.wide.at[peer], self.send.at[4, 0], self.receive.at[4, peer], partner()) for peer, _ in found
            ]
            self.end(copies, arrivals)
            total = self.wide[0].astype(f32)
            for rank in range(1, self.links.extra):
                total = total + self.wide[rank].astype(f32)
        rows = self.span(self.start_of(3), self.third)
        self.result[0, rows, :] = total.astype(bf16)
        self.moment_out[...] = (muon_decay * old[rows, :] + total).astype(bf16)
        self.run([self.pair_copy(5, self.moment_out, self.moment_in)])

    def gather(self, phase, slot, depth, size):
        mine = self.start_of(depth)
        me = self.rank(slot)
        copies, arrivals = [], []
        for step, peer in enumerate(self.links.stage_peers(slot)):
            device = self.links.stage_id(slot, peer)
            rows = self.span(mine, size)
            theirs = self.span(mine + (peer - me) * size, size)
            copies.append(
                remote(self.result.at[:, rows, :], self.result.at[:, rows, :], self.send.at[phase, step], self.receive.at[phase, me], device)
            )
            arrivals.append(
                remote(self.result.at[:, theirs, :], self.result.at[:, theirs, :], self.send.at[phase, step], self.receive.at[phase, peer], device)
            )
        return copies, arrivals

    def scattered(self):
        copies = [self.pair_copy(5, self.moment_out, self.moment_in)]
        self.end(copies, copies)
        self.result[1, self.span(self.start_of(3), self.third), :] = self.moment_in[...]

    def begin_gather(self):
        self.run(self.gather(6, 2, 3, self.third)[0])

    def step5(self):
        self.scattered()
        self.begin_gather()

    def step6(self):
        self.end(*self.gather(6, 2, 3, self.third))
        self.run(self.gather(7, 1, 2, self.second)[0])

    def step7(self):
        self.end(*self.gather(7, 1, 2, self.second))
        self.run(self.gather(8, 0, 1, self.first)[0])

    def step8(self):
        self.end(*self.gather(8, 0, 1, self.first))


class Quick:
    def __init__(self, links, rows, refs):
        self.links, self.size = links, rows // links.split
        self.g, self.near_in, self.far, self.moment, self.result, self.send, self.receive = refs

    @staticmethod
    def scratch(links, rows):
        size = rows // links.split
        slots = max(links.near, links.far)
        return [
            pltpu.VMEM((2, rows, 128), bf16),
            pltpu.VMEM((links.near, size, 128), bf16),
            pltpu.VMEM((links.far, size, 128), bf16),
            pltpu.VMEM((size, 128), bf16),
            pltpu.VMEM((2, rows, 128), bf16),
            pltpu.SemaphoreType.DMA((3, slots)),
            pltpu.SemaphoreType.DMA((3, slots)),
        ]

    def rows_of(self, rank):
        return pl.ds(pl.multiple_of(lax.rem(rank, self.links.split) * self.size, 16), self.size)

    def side_of(self, rank):
        _, mp, _, _ = self.links.here()
        there = lax.div(rank, self.links.split)
        return there + mp - 2 * there * mp

    def me(self):
        _, mp, low, high = self.links.here()
        return mp * self.links.split + low, high

    def near_copy(self, step, peer):
        me, _ = self.me()
        source = self.g.at[self.side_of(peer), self.rows_of(peer), :]
        return remote(source, self.near_in.at[me], self.send.at[0, step], self.receive.at[0, me], self.links.near_id(peer))

    def far_copy(self, step, peer):
        _, high = self.me()
        slot = self.far.at[high]
        return remote(slot, slot, self.send.at[1, step], self.receive.at[1, high], self.links.far_id(peer))

    def wait(self, phase, peers, slots, copies, ids):
        for peer in peers:
            remote(slots.at[peer], slots.at[peer], self.send.at[phase, 0], self.receive.at[phase, peer], ids(peer)).wait_recv()
        for copy in copies:
            copy.wait_send()

    def start(self):
        for step, peer in enumerate(self.links.near_peers()):
            self.near_copy(step, peer).start()

    def cross(self):
        peers = self.links.near_peers()
        self.wait(0, peers, self.near_in, [self.near_copy(step, peer) for step, peer in enumerate(peers)], self.links.near_id)
        me, high = self.me()
        total = self.g[0, self.rows_of(me), :].astype(f32)
        for peer in peers:
            total = total + self.near_in[peer].astype(f32)
        self.far[high] = total.astype(bf16)
        for step, peer in enumerate(self.links.far_peers()):
            self.far_copy(step, peer).start()

    def back_copy(self, step, peer):
        me, _ = self.me()
        rows = self.rows_of(me)
        side = self.side_of(peer)
        target = self.result.at[side, rows, :]
        own = remote(self.result.at[0, rows, :], target, self.send.at[2, step], self.receive.at[2, me], self.links.near_id(peer))
        other = remote(self.moment, target, self.send.at[2, step], self.receive.at[2, me], self.links.near_id(peer))
        return side, own, other

    def back(self, old):
        peers = self.links.far_peers()
        self.wait(1, peers, self.far, [self.far_copy(step, peer) for step, peer in enumerate(peers)], self.links.far_id)
        total = self.far[0].astype(f32)
        for rank in range(1, self.links.far):
            total = total + self.far[rank].astype(f32)
        me, _ = self.me()
        rows = self.rows_of(me)
        self.result[0, rows, :] = total.astype(bf16)
        self.moment[...] = (muon_decay * old[rows, :] + total).astype(bf16)
        for step, peer in enumerate(self.links.near_peers()):
            side, own, other = self.back_copy(step, peer)
            pl.when(side == 0)(own.start)
            pl.when(side == 1)(other.start)

    def finish(self):
        for peer in self.links.near_peers():
            rows = self.rows_of(peer)
            arrival = self.result.at[self.side_of(peer), rows, :]
            remote(arrival, arrival, self.send.at[2, 0], self.receive.at[2, peer], self.links.near_id(peer)).wait_recv()
        for step, peer in enumerate(self.links.near_peers()):
            self.back_copy(step, peer)[1].wait_send()


def split(value):
    high = value.astype(bf16)
    return (high, (value - high.astype(f32)).astype(bf16))


def wide_dot(left, right):
    return dot(left[0], right[0]) + (dot(left[0], right[1]) + dot(left[1], right[0]))


def gram_of(own, other, tall):
    if tall:
        own, other = own.reshape(-1, own.shape[2]), other.reshape(-1, own.shape[2])
        cross = t_dot(own, other)
        top = jnp.concatenate([t_dot(own, own), cross], axis=1)
        bottom = jnp.concatenate([cross.T, t_dot(other, other)], axis=1)
        return jnp.concatenate([top, bottom], axis=0)
    gram = None
    for half in (own, other):
        for group in range(own.shape[0]):
            part = dot_t(half[group], half[group])
            gram = part if gram is None else gram + part
    return gram


def schulz(grams):
    identities, scales, states = [], [], []
    for gram in grams:
        size = gram.shape[0]
        row_ids = lax.broadcasted_iota(jnp.int32, (size, size), 0)
        col_ids = lax.broadcasted_iota(jnp.int32, (size, size), 1)
        identity = (row_ids == col_ids).astype(f32)
        trace = jnp.sum(jnp.sum(gram * identity, axis=0, keepdims=True), axis=1, keepdims=True)
        scale = 1.0 / (jnp.sqrt(trace) + 1e-07)
        identities.append(identity)
        scales.append(scale)
        states.append(gram * (scale * scale))
    products = [None] * len(grams)
    for sweep in range(5):
        halves = [split(state) for state in states]
        squares = [wide_dot(half, half) for half in halves]
        polynomials = [
            schulz_coeffs[0] * identity + (schulz_coeffs[1] * state + schulz_coeffs[2] * square)
            for identity, state, square in zip(identities, states, squares)
        ]
        factors = [split(polynomial) for polynomial in polynomials]
        if sweep == 0:
            products = polynomials
        else:
            products = [wide_dot(factor, split(product)) for factor, product in zip(factors, products)]
        if sweep < 4:
            firsts = [wide_dot(factor, half) for factor, half in zip(factors, halves)]
            states = [wide_dot(split(first), factor) for first, factor in zip(firsts, factors)]
        yield
    return [product * scale for product, scale in zip(products, scales)]


def drain(work):
    while True:
        try:
            next(work)
        except StopIteration as stop:
            return stop.value


def muon_kernel(factors, talls, known, held, *refs):
    size = len(factors)
    reduced, refs = refs[: len(held)], refs[len(held) :]
    olds, weights, refs = refs[:size], refs[size : 2 * size], refs[2 * size :]
    known_refs, refs = refs[:known], refs[known:]
    moments, nexts, copies = refs[:size], refs[size : 2 * size], refs[2 * size :]
    owns, others = [], []
    for source, many in zip(reduced, held):
        start = 0
        for _ in range(many):
            slot = len(owns)
            shape = olds[slot].shape
            rows = slice(start, start + shape[0] * shape[1])
            start = rows.stop
            moment = muon_decay * olds[slot][...] + source[0, rows, :].astype(f32).reshape(shape)
            moments[slot][...] = moment
            owns.append(moment.astype(bf16))
            others.append(source[1, rows, :].reshape(shape))
    grams = [gram_of(owns[slot], others[slot], talls[slot]) for slot in range(known, size)]
    products = [ref[...].astype(bf16) for ref in known_refs]
    products += [product.astype(bf16) for product in drain(schulz(grams))]
    for slot in range(size):
        product, own, other = products[slot], owns[slot], others[slot]
        half = own.shape[2]
        for group in range(own.shape[0]):
            if talls[slot]:
                shaped = dot(own[group], product[:half, :half]) + dot(other[group], product[half:, :half])
            else:
                shaped = dot(product, own[group])
            result = weights[slot][group] - muon_rate * factors[slot] * shaped
            nexts[slot][group] = result
            copies[slot][group] = result.astype(bf16)


def muon_update(reduced, held, olds, weights, talls, products):
    factors = []
    for weight, tall in zip(weights, talls):
        columns = 2 * weight.shape[2]
        matrix_rows = weight.shape[0] * weight.shape[1] if tall else weight.shape[1]
        matrix_columns = columns if tall else weight.shape[0] * columns
        factors.append(max(1.0, matrix_rows / matrix_columns) ** 0.5)
    outs = pl.pallas_call(
        functools.partial(muon_kernel, factors, talls, len(products), held),
        out_shape=tuple(jax.ShapeDtypeStruct(w.shape, kind) for kind in (f32, f32, bf16) for w in weights),
        compiler_params=params_of(),
        name="muon",
    )(*reduced, *olds, *weights, *products)
    count = len(weights)
    return outs[:count], outs[count : 2 * count], outs[2 * count :]


def time_weights(grad_t, extended, grad_ref, tap, stride, reach):
    chunks, _, chunk_rows = grad_t.shape
    lo_count = LO // chunks
    parity, shift = taps(stride)[tap]
    result = None
    for chunk in range(chunks):
        start = reach + shift + chunk * lo_count
        hidden = extended[parity][start : start + lo_count].reshape(chunk_rows, -1)
        part = dot(grad_t[chunk], hidden)
        result = part if result is None else result + part
    give_gradient(grad_ref, tap * result.shape[0], result.T, result.shape[0] // 2)


def turn(source, grad_t, reach):
    chunks, channels, chunk_rows = grad_t.shape
    lo_count = LO // chunks
    for chunk in range(chunks):
        start = reach + chunk * lo_count
        grad_t[chunk] = source[start : start + lo_count].reshape(chunk_rows, channels).T


def packed_edges(edges):
    joints = edges.shape[1]
    total = jnp.sum(jnp.sum(edges[...], axis=2), axis=2, keepdims=True)
    joint_ids = lax.broadcasted_iota(jnp.int32, (3, joints, 128), 1)
    lane_ids = lax.broadcasted_iota(jnp.int32, (3, joints, 128), 2)
    return jnp.sum(jnp.where(joint_ids == lane_ids, total, 0.0), axis=1)


def backward_kernel(
    links, joints, length,
    up_in, temporal_two_in, spatial_two_in, middle_in, temporal_in, skipped_in, spatial_in, x_in, time_two_in, graph_two_in, time_one_in,
    time_two_old_in, graph_two_old_in, time_one_old_in,
    graph_one_own, graph_one_other, skip_own, skip_other, skip_old, graph_one_old, norm_ref, parent_ref, children_ref, first_values, second_values,
    total1_ref, total2_ref, total3_ref, total4_ref, total5_ref,
    keep_out, early_received, late_received, time_two_out, graph_two_out, time_one_out, small_out, product_time, product_graph,
    total6_ref, total7_ref, total8_ref, edge_total,
    up, temporal_two, spatial_two, middle, temporal, skipped, spatial, x, time_two, graph_two, time_one,
    time_two_old, graph_two_old, time_one_old, small_old,
    gradient, hidden, grad_t, product, stat_ref, sums_ref,
    gradient_lo, spread_two, mixed_two, scaled, scaled_back, inward, up_sum, down_sum, in_sum, out_sum,
    graph_two_total, edges_two, skip_total,
    gradient_pair, strided, graph_one_total, edges_one, graph_one, skip_one,
    load_sem, store_sem, drip_send, drip_receive, *refs,
):
    rows, channels = up.shape[1:]
    width = x.shape[-1]
    thin = width // 2
    frame_length = length[0]
    norm = norm_ref[...]
    count = total1_ref[5:6, :]
    half = LO // 2
    first_tree = Tree((parent_ref, children_ref, first_values))
    second_tree = Tree((parent_ref, children_ref, second_values))
    reducers = []
    for old in (time_two_old, graph_two_old, time_one_old):
        size = len(Reducer.scratch(links, 256))
        reducers.append(Reducer(links, old.shape[0], refs[:size]))
        refs = refs[size:]
    size = len(Quick.scratch(links, 256))
    quick, refs = Quick(links, small_old.shape[0], refs[:size]), refs[size:]
    per_sum = len(refs) // 4
    sum6, sum7, sum8 = [Sum(links, refs[slot * per_sum : (slot + 1) * per_sum]) for slot in range(3)]
    edge_sum = Sum(links, refs[3 * per_sum :], halves=False)
    for_time_two, for_graph_two, for_time_one = reducers
    reach_one = LO + 4
    hidden_two = [hidden.at[0 : LO + 8]]
    hidden_one = [hidden.at[0:reach_one], hidden.at[reach_one : 2 * reach_one]]
    keep = hidden.at[0:LO, :, 0:width]
    early = hidden.at[reach_one : reach_one + half, :, 0:width]
    late = hidden.at[reach_one + half : reach_one + 2 * half, :, 0:width]
    early_drip = Drip(early, early_received, drip_send, drip_receive)
    late_drip = Drip(late, late_received, drip_send, drip_receive, half)

    pairs = (
        (up_in, up), (temporal_two_in, temporal_two), (time_two_in, time_two), (spatial_two_in, spatial_two), (graph_two_in, graph_two),
        (middle_in, middle), (temporal_in, temporal), (skipped_in, skipped), (spatial_in, spatial), (x_in, x), (time_one_in, time_one),
        (time_two_old_in, time_two_old), (graph_two_old_in, graph_two_old), (time_one_old_in, time_one_old),
    )
    loads = [pltpu.make_async_copy(source, target, load_sem.at[slot]) for slot, (source, target) in enumerate(pairs)]
    stores = [
        pltpu.make_async_copy(source, target, store_sem.at[slot])
        for slot, (source, target) in enumerate(
            (
                (keep, keep_out), (for_time_two.result, time_two_out), (for_graph_two.result, graph_two_out), (for_time_one.result, time_one_out),
                (quick.result, small_out),
            )
        )
    ]
    links.greet()
    for load in loads:
        load.start()
    assemble(graph_one, graph_one_own, graph_one_other, thin)
    assemble(skip_one, skip_own, skip_other, thin)
    small_old[0 : skip_old.shape[0], :] = skip_old[...]
    small_old[skip_old.shape[0] :, :] = graph_one_old[...]
    for ref in (stat_ref, sums_ref, graph_two_total, edges_two, skip_total, graph_one_total, edges_one):
        ref[...] = jnp.zeros_like(ref)

    loads[0].wait()
    loads[1].wait()
    rows4 = norm_rows(total4_ref[...], 0, count, norm, 4)
    of_grad4, of_value4, constant4 = backward_rows(rows4, count, total5_ref[0:1, :], total5_ref[1:2, :])
    for part in range(2):
        place = slice(part * half, (part + 1) * half)
        mask = half_mask(part * half, half, frame_length, channels)

        def gradient_two(joint, _):
            where = joint_rows(joint)
            value = up[place, where, :].astype(f32) * of_grad4 + (temporal_two[place, where, :].astype(f32) * of_value4 + constant4)
            put_with_halo(gradient, part * half, half, 4, where, value * mask)
            return 0

        lax.fori_loop(0, joints, gradient_two, 0)

    zero = jnp.zeros((8, channels), f32)

    def through_silu(values, normed_of, gain, bias, target, extended, reach, part, parity, keep_hidden):
        place = slice(part * half, (part + 1) * half)
        mask = half_mask(part * half, half, frame_length, channels, parity)
        inverse, offset = normed_of

        def body(joint, carry):
            where = joint_rows(joint)
            normed = values[place, where, :].astype(f32) * inverse + offset
            pre = normed * gain + bias
            gate = sigmoid(pre)
            active = pre * gate
            if keep_hidden:
                put_with_halo(extended, part * half, half, reach, where, active * mask)
            grad = product[:, where, :] * mask * (gate + active * (1.0 - gate))
            target[place, where, :] = grad.astype(bf16)
            return (carry[0] + fold(grad), carry[1] + fold(grad * normed))

        found = lax.fori_loop(0, joints, body, (zero, zero))
        stat_ref[0:1, :] += row_sum(found[0])
        stat_ref[1:2, :] += row_sum(found[1])

    rows3 = norm_rows(total3_ref[...], 0, count, norm, 3)
    loads[2].wait()
    loads[3].wait()
    pre_three = temporal_two
    for part in range(2):

        def multiply_two(index, _):
            product[index] = time_backward(gradient, time_two, part * half + index, 1, 4, 0)
            return 0

        lax.fori_loop(0, half, multiply_two, 0)
        through_silu(spatial_two, normed_rows(rows3), rows3[2], rows3[3], pre_three, hidden_two[0], 4, part, 0, True)

    links.meet()
    sum6.start_near(stat_ref[0:2, :])
    turn(gradient, grad_t, 4)
    for tap in range(9):
        if tap == 4:
            sum6.start_far()
        time_weights(grad_t, hidden_two, for_time_two.g, tap, 1, 4)
    for_time_two.step0()
    total6_ref[0:2, :] = sum6.total()

    for slot in (4, 5, 6, 7):
        loads[slot].wait()
    of_grad3, of_value3, constant3 = backward_rows(rows3, count, total6_ref[0:1, :], total6_ref[1:2, :])
    rows2 = norm_rows(total2_ref[...], 0, count, norm, 1)
    rows_s = norm_rows(total1_ref[...], 2, count, norm, 2)
    inverse2, offset2 = normed_rows(rows2)
    inverse_s, offset_s = normed_rows(rows_s)
    gain2, gain_s, join_bias = rows2[2], rows_s[2], rows2[3] + rows_s[3]
    joined = spatial_two

    def middle_body(lo, _):
        mask = chunk_mask(lo, frame_length, channels)
        for chunk, where in chunks(rows):
            value = pre_three[lo, where, :].astype(f32) * of_grad3 + (spatial_two[lo, where, :].astype(f32) * of_value3 + constant3)
            gradient_lo[where, :] = (value * mask).astype(bf16)
            value = middle[lo, where, :].astype(f32)
            scaled[where, :] = second_tree.scale(value, 1, chunk).astype(bf16)
            mixed_two[where, 0:channels] = second_tree.scale(value, 0, chunk).astype(bf16)
        up_sum[...] = dot(parent_ref[...], middle[lo])
        down_sum[...] = dot(children_ref[...], scaled[...])
        spread_two[...] = dot_t(gradient_lo[...], graph_two[...].reshape(-1, channels))
        for chunk, where in chunks(rows):
            inward[where, :] = spread_two[where, channels : 2 * channels].astype(bf16)
            scaled_back[where, :] = second_tree.scale(spread_two[where, 2 * channels : 3 * channels], 2, chunk).astype(bf16)
            mixed_two[where, channels : 2 * channels] = down_sum[where, :].astype(bf16)
            mixed_two[where, 2 * channels : 3 * channels] = second_tree.scale(up_sum[where, :], 2, chunk).astype(bf16)
        in_sum[...] = dot(parent_ref[...], inward[...])
        out_sum[...] = dot(children_ref[...], scaled_back[...])
        graph_two_total[...] += t_dot(gradient_lo[...], mixed_two[...])
        for chunk, where in chunks(rows):
            some = slice(chunk * CHUNK, (chunk + 1) * CHUNK)
            value = middle[lo, where, :].astype(f32)
            own, from_parent = spread_two[where, 0:channels], in_sum[where, :]
            edges_two[0, some] += fold_joints(value * own)
            edges_two[1, some] += fold_joints(value * from_parent)
            edges_two[2, some] += fold_joints(up_sum[where, :] * spread_two[where, 2 * channels : 3 * channels])
            through_graph = second_tree.scale(own, 0, chunk) + second_tree.scale(from_parent, 1, chunk) + out_sum[where, :]
            normed2 = temporal[lo, where, :].astype(f32) * inverse2 + offset2
            normed_s = skipped[lo, where, :].astype(f32) * inverse_s + offset_s
            pre = normed2 * gain2 + (normed_s * gain_s + join_bias)
            gate = sigmoid(pre)
            grad = (through_graph + up[lo, where, :].astype(f32)) * mask * (gate + pre * gate * (1.0 - gate))
            joined[lo, where, :] = grad.astype(bf16)
            sums_ref[0] += fold(grad)
            sums_ref[1] += fold(grad * normed2)
            sums_ref[2] += fold(grad * normed_s)
        pl.when(lo == 1)(for_time_two.step1)
        pl.when(lo == 7)(for_time_two.step2)
        return 0

    lax.fori_loop(0, LO, middle_body, 0)
    for slot in range(3):
        stat_ref[slot : slot + 1, :] = row_sum(sums_ref[slot])
    sum7.start_near(stat_ref[0:3, :])
    result = graph_two_total[...].T
    for group in range(3):
        give_gradient(for_graph_two.g, group * channels, result[group * channels : (group + 1) * channels], channels // 2)
    for_graph_two.step0()

    loads[8].wait()
    scale1, shift1 = forward_rows(norm_rows(total1_ref[...], 0, total1_ref[4:5, :], norm, 0))
    for parity in range(2):
        for part in range(2):
            mask = half_mask(part * half, half, frame_length, channels, parity)

            def again(joint, _):
                where = joint_rows(joint)
                pre = spatial[parity, part * half : (part + 1) * half, where, :].astype(f32) * scale1 + shift1
                put_with_halo(hidden_one[parity], part * half, half, 2, where, pre * sigmoid(pre) * mask)
                return 0

            lax.fori_loop(0, joints, again, 0)
            if (parity, part) == (0, 1):
                sum7.start_far()
                for_graph_two.step1()
    total7_ref[0:3, :] = sum7.total()
    for_time_two.step3()

    loads[9].wait()
    loads[10].wait()
    bias_grad = total7_ref[0:1, :]
    grad2, value2, constant2 = backward_rows(rows2, count, bias_grad, total7_ref[1:2, :])
    grad_s, value_s, constant_s = backward_rows(rows_s, count, bias_grad, total7_ref[2:3, :])
    skip_grad = skipped
    for part in range(2):
        place = slice(part * half, (part + 1) * half)
        mask = half_mask(part * half, half, frame_length, channels)

        def gradient_one(joint, _):
            where = joint_rows(joint)
            value = joined[place, where, :].astype(f32)
            into_two = value * grad2 + (temporal[place, where, :].astype(f32) * value2 + constant2)
            put_with_halo(gradient, part * half, half, 2, where, into_two * mask)
            into_skip = value * grad_s + (skipped[place, where, :].astype(f32) * value_s + constant_s)
            skip_grad[place, where, :] = (into_skip * mask).astype(bf16)
            return 0

        lax.fori_loop(0, joints, gradient_one, 0)
        skip_total[...] += t_dot(x[0, place].reshape(-1, width), skip_grad[place].reshape(-1, channels))
    for slot in (11, 12, 13):
        loads[slot].wait()
    for_time_two.step4(time_two_old)
    for_graph_two.step2()

    stat_ref[...] = jnp.zeros_like(stat_ref)
    rows1 = norm_rows(total1_ref[...], 0, total1_ref[4:5, :], norm, 0)
    pre_one = (up, middle)
    for parity in range(2):
        for part in range(2):

            def multiply_one(index, _):
                product[index] = time_backward(gradient, time_one, part * half + index, 2, 2, parity)
                return 0

            lax.fori_loop(0, half, multiply_one, 0)
            if (parity, part) == (0, 0):
                for_time_two.step5()
                for_graph_two.step3()
            if (parity, part) == (0, 1):
                for_graph_two.step4(graph_two_old)
            if (parity, part) == (1, 0):
                for_time_two.step6()
                for_graph_two.step5()
            through_silu(spatial.at[parity], normed_rows(rows1), rows1[2], rows1[3], pre_one[parity], None, 2, part, parity, False)

    sum8.start_near(stat_ref[0:2, :])
    give_gradient(quick.g, 0, skip_total[...], thin)
    turn(gradient, grad_t, 2)
    for tap in range(9):
        if tap == 5:
            sum8.start_far()
            for_time_two.step7()
            for_graph_two.step6()
        time_weights(grad_t, hidden_one, for_time_one.g, tap, 2, 2)
    total8_ref[0:2, :] = sum8.total()
    for_time_one.step0()
    for_time_two.step8()
    for_graph_two.step7()
    stores[1].start()

    of_grad1, of_value1, constant1 = backward_rows(rows1, total1_ref[4:5, :], total8_ref[0:1, :], total8_ref[1:2, :])
    lanes = lax.broadcasted_iota(jnp.int32, (CHUNK * PAD, width), 1)
    spot = lambda index, where: slice(index * rows + where.start, index * rows + where.stop)
    third = lambda index, start, count: slice((3 * index + start) * width, (3 * index + start + count) * width)
    for parity in range(2):

        def input_body(pair, _):
            pick = lambda index, where: x[parity, 2 * pair + index, where, :]
            for index in range(2):
                lo = 2 * pair + index
                mask = chunk_mask(lo, frame_length, channels, parity)
                for chunk, where in chunks(rows):
                    value = pre_one[parity][lo, where, :].astype(f32) * of_grad1
                    value = value + (spatial[parity, lo, where, :].astype(f32) * of_value1 + constant1)
                    gradient_pair[spot(index, where), :] = (value * mask).astype(bf16)
            for chunk, where in chunks(rows):
                both = jnp.concatenate([pick(0, where), pick(1, where)], axis=1).astype(f32)
                scaled[where, :] = first_tree.scale(both, 1, chunk).astype(bf16)
            both = jnp.concatenate([pick(0, slice(0, rows)), pick(1, slice(0, rows))], axis=1)
            up_sum[...] = dot(parent_ref[...], both)
            down_sum[...] = dot(children_ref[...], scaled[...])
            for index in range(2):
                whole_lo = slice(index * rows, (index + 1) * rows)
                spread_two[:, third(index, 0, 3)] = dot_t(gradient_pair[whole_lo, :], graph_one[...].reshape(-1, channels))
            if parity == 0:
                strided[...] = dot_t(skip_grad[pl.ds(2 * pair, 2)].reshape(2 * rows, channels), skip_one[0])
            for index in range(2):
                columns = slice(index * width, (index + 1) * width)
                for chunk, where in chunks(rows):
                    inward[where, columns] = spread_two[where, third(index, 1, 1)].astype(bf16)
                    scaled_back[where, columns] = first_tree.scale(spread_two[where, third(index, 2, 1)], 2, chunk).astype(bf16)
                    mixed_two[where, third(index, 0, 1)] = first_tree.scale(pick(index, where).astype(f32), 0, chunk).astype(bf16)
                    mixed_two[where, third(index, 1, 1)] = down_sum[where, columns].astype(bf16)
                    mixed_two[where, third(index, 2, 1)] = first_tree.scale(up_sum[where, columns], 2, chunk).astype(bf16)
            in_sum[...] = dot(parent_ref[...], inward[...])
            out_sum[...] = dot(children_ref[...], scaled_back[...])
            for index in range(2):
                whole_lo = slice(index * rows, (index + 1) * rows)
                graph_one_total[...] += t_dot(gradient_pair[whole_lo, :], mixed_two[:, third(index, 0, 3)])
            masks = [chunk_mask(2 * pair + index, frame_length, width, parity) for index in range(2)]
            for chunk, where in chunks(rows):
                some = slice(chunk * CHUNK, (chunk + 1) * CHUNK)
                totals = []
                for index in range(2):
                    columns = slice(index * width, (index + 1) * width)
                    place = spot(index, where)
                    value = pick(index, where).astype(f32)
                    own, from_parent = spread_two[where, third(index, 0, 1)], in_sum[where, columns]
                    edges_one[0, some] += fold_joints(value * own)
                    edges_one[1, some] += fold_joints(value * from_parent)
                    edges_one[2, some] += fold_joints(up_sum[where, columns] * spread_two[where, third(index, 2, 1)])
                    total = first_tree.scale(own, 0, chunk) + first_tree.scale(from_parent, 1, chunk) + out_sum[where, columns]
                    if parity == 0:
                        total = total + strided[place, :]
                    totals.append(total * masks[index])
                even, odd = totals
                send = early if parity == 0 else late
                keep[parity * half + pair, where, :] = jnp.where(lanes < thin, even, pltpu.roll(odd, thin, 1)).astype(bf16)
                send[pair, where, :] = jnp.where(lanes < thin, pltpu.roll(even, thin, 1), odd).astype(bf16)
            if parity == 0:
                pl.when(pair == 0)(for_graph_two.step8)
                pl.when(pair == 1)(for_time_one.step1)
                pl.when(pair == 4)(for_time_one.step2)
            else:
                early_drip.start(pair)
                pl.when(pair == 1)(for_time_one.step3)
                pl.when(pair == 3)(lambda: for_time_one.step4(time_one_old))
            return 0

        lax.fori_loop(0, half, input_body, 0)
        if parity == 0:
            stores[2].start()

    result = graph_one_total[...].T
    for group in range(3):
        give_gradient(quick.g, skip_old.shape[0] + group * width, result[group * width : (group + 1) * width], thin)
    quick.start()
    stat_ref[0:3, 0:128] = packed_edges(edges_one)
    stat_ref[3:6, 0:128] = packed_edges(edges_two)
    edge_sum.start_near(stat_ref[0:6, 0:128])
    for_time_one.step5()
    stores[0].start()

    def second_work():
        grams = []
        for old, reducer, groups, tall in ((time_two_old, for_time_two, 9, True), (graph_two_old, for_graph_two, 3, False)):
            shape = (groups, old.shape[0] // groups, 128)
            own = (muon_decay * old[...] + reducer.result[0].astype(f32)).astype(bf16)
            grams.append(gram_of(own.reshape(shape), reducer.result[1].reshape(shape), tall))
        yield
        found = yield from schulz(grams)
        product_time[...], product_graph[...] = found

    work = second_work()
    next(work)
    quick.cross()
    edge_sum.start_far()
    next(work)
    quick.back(small_old)
    next(work)
    for_time_one.step6()
    edge_total[0:6, :] = edge_sum.total()
    edge_total[6:8, :] = jnp.zeros((2, 128), f32)
    for index in range(half):
        late_drip.start(index)
    next(work)
    quick.finish()
    stores[4].start()
    next(work)
    next(work)
    for _ in work:
        pass
    for_time_one.step7()
    for_time_one.step8()
    stores[3].start()
    early_drip.wait()
    late_drip.wait()
    for store in stores:
        store.wait()


def backward_stage(links, length, activations, weights, big_olds, small, small_olds, norm, first_tree, second_tree, totals):
    up, _, _, _, _, _, spatial, x = activations
    rows, channels = up.shape[1:]
    width = x.shape[-1]
    joints = rows // PAD
    half = LO // 2
    vmem = pl.BlockSpec(memory_space=pltpu.VMEM)
    pairs = (half, rows, width)
    small_rows = sum(old.shape[0] for old in small_olds)
    reduced = [(2,) + old.shape for old in big_olds] + [(2, small_rows, 128)]
    wide, narrow = pltpu.VMEM((rows, channels), f32), pltpu.VMEM((rows, channels), bf16)
    sum_shapes = ((2, channels), (3, channels), (2, channels), (6, 128))
    outs = pl.pallas_call(
        functools.partial(backward_kernel, links, joints),
        out_shape=[jax.ShapeDtypeStruct((LO, rows, width), bf16), jax.ShapeDtypeStruct(pairs, bf16), jax.ShapeDtypeStruct(pairs, bf16)]
        + [jax.ShapeDtypeStruct(shape, bf16) for shape in reduced]
        + [jax.ShapeDtypeStruct((channels, channels), f32)] * 2
        + [jax.ShapeDtypeStruct((8, channels), f32)] * 3
        + [jax.ShapeDtypeStruct((8, 128), f32)],
        in_specs=[smem()] + [anywhere()] * 14 + [vmem] * 16,
        out_specs=[anywhere()] * 7 + [vmem] * 6,
        scratch_shapes=[pltpu.VMEM(tensor.shape, bf16) for tensor in tuple(activations) + tuple(weights)]
        + [pltpu.VMEM(old.shape, f32) for old in big_olds]
        + [
            pltpu.VMEM((small_rows, 128), f32),
            pltpu.VMEM((LO + 8, rows, channels), bf16),
            pltpu.VMEM((2 * LO + 8, rows, channels), bf16),
            pltpu.VMEM((2, channels, half * rows), bf16),
            pltpu.VMEM((half, rows, channels), f32),
            pltpu.VMEM((8, channels), f32),
            pltpu.VMEM((3, 8, channels), f32),
            narrow,
            pltpu.VMEM((rows, 3 * channels), f32),
            pltpu.VMEM((rows, 3 * channels), bf16),
            narrow,
            narrow,
            narrow,
            wide,
            wide,
            wide,
            wide,
            pltpu.VMEM((channels, 3 * channels), f32),
            pltpu.VMEM((3, joints, 8, channels), f32),
            pltpu.VMEM((width, channels), f32),
            pltpu.VMEM((2 * rows, channels), bf16),
            pltpu.VMEM((2 * rows, width), f32),
            pltpu.VMEM((channels, 3 * width), f32),
            pltpu.VMEM((3, joints, 8, width), f32),
            pltpu.VMEM((3, width, channels), bf16),
            pltpu.VMEM((1, width, channels), bf16),
            pltpu.SemaphoreType.DMA((14,)),
            pltpu.SemaphoreType.DMA((5,)),
            pltpu.SemaphoreType.DMA((2 * half,)),
            pltpu.SemaphoreType.DMA((2 * half,)),
        ]
        + [scratch for old in big_olds for scratch in Reducer.scratch(links, old.shape[0])]
        + Quick.scratch(links, small_rows)
        + [scratch for shape in sum_shapes for scratch in links.sum_scratch(shape)],
        compiler_params=remote_params("backward"),
        name="backward",
    )(
        length, *activations, *weights, *big_olds, *small[0], *small[1], *small_olds, norm,
        first_tree[0], first_tree[1], first_tree[2], second_tree[2], *totals,
    )
    return outs


def tree_values(parents):
    joints = parents.shape[0]
    ids = jnp.arange(joints, dtype=jnp.int32)
    child = ids > 0
    edge = (parents[:, None] == ids[None, :]) & child[:, None]
    degree = (1 + jnp.sum(edge, axis=0) + child).astype(f32)
    inverse = 1.0 / degree
    placed = jnp.stack([ids[:, None] == ids[None, :], edge, edge.T])
    hi_ids = jnp.arange(joints * PAD, dtype=jnp.int32) % PAD
    target = jnp.where(jnp.repeat(child, PAD), jnp.repeat(parents, PAD) * PAD + hi_ids, -1)
    row_ids = jnp.arange(joints * PAD, dtype=jnp.int32)
    parent = (target[:, None] == row_ids[None, :]).astype(bf16)
    children = (row_ids[:, None] == target[None, :]).astype(bf16)
    return placed, inverse, parent, children


def per_device(
    links,
    clips,
    lengths,
    grad_out,
    parents,
    first_graph,
    first_time,
    first_skip,
    second_graph,
    second_time,
    first_graph_moment,
    first_time_moment,
    first_skip_moment,
    second_graph_moment,
    second_time_moment,
    norm_param,
    norm_moment,
    edge_weight,
    edge_moment,
):
    half_index = lax.axis_index("mp")
    frame_count, joints, thin = clips.shape[1:]
    half_count = frame_count // 2
    hi_count = half_count // LO
    local = first_time.shape[2]
    rows = joints * PAD

    def pick(tensor, index):
        return lax.dynamic_index_in_dim(tensor, index, 0, keepdims=False)

    def by_group(weight):
        return jnp.transpose(weight, (1, 0, 2))

    def exchange(tensor):
        return lax.ppermute(tensor, "mp", [(0, 1), (1, 0)])

    length = pick(lengths, half_index).reshape(1)
    frames = jnp.transpose(clips, (0, 2, 3, 1))
    other_frames = exchange(pick(frames, 1 - half_index))

    weights = (by_group(first_graph), first_time, first_skip[None], by_group(second_graph), second_time)
    graph_one_own, time_one_own, skip_one_own, graph_two_own, time_two_own = [weight.astype(bf16) for weight in weights]
    norm_own = jnp.pad(norm_param, ((0, 0), (0, 3), (0, 0))).reshape(16, local)

    def cotangent_layout(tensor):
        tensor = jnp.transpose(tensor.reshape(2, hi_count, LO, joints, local), (0, 2, 3, 1, 4))
        return jnp.pad(tensor, ((0, 0), (0, 0), (0, 0), (0, PAD - hi_count), (0, 0))).reshape(2, LO, rows, local)

    cotangents = cotangent_layout(grad_out)
    cotangent_own, cotangent_other = pick(cotangents, half_index), pick(cotangents, 1 - half_index)

    placed, inverse, parent, children = tree_values(parents)
    edge_placed = jnp.where(placed[None], edge_weight, 0.0) * inverse[None, None, None, :]
    graph_values = jnp.stack(
        [jnp.sum(edge_placed[:, 0], axis=1), jnp.sum(edge_placed[:, 1], axis=2), jnp.sum(edge_placed[:, 2], axis=1)], axis=1
    )
    graph_rows = jnp.broadcast_to(graph_values[:, :, :, None, None], (2, 3, joints, 8, 128))
    (
        other_frames, graph_one_own, time_one_own, skip_one_own, graph_two_own, time_two_own, norm_own,
        cotangent_own, cotangent_other, parent, children, first_values, second_values, length,
    ) = lax.optimization_barrier(
        (
            other_frames, graph_one_own, time_one_own, skip_one_own, graph_two_own, time_two_own, norm_own,
            cotangent_own, cotangent_other, parent, children, graph_rows[0], graph_rows[1], length,
        )
    )
    first_tree, second_tree = (parent, children, first_values), (parent, children, second_values)

    clip, graph_one_other, skip_one_other, norm = frames_in(links, frames, other_frames, length, graph_one_own, skip_one_own, norm_own)
    graph_one, skip_one = (graph_one_own, graph_one_other), (skip_one_own, skip_one_other)
    (
        (
            spatial, skipped, temporal, middle, spatial_two, temporal_two, up, block_own, block_other, time_one, graph_two, time_two
        ),
        (total1, total2, total3, total4, total5),
    ) = forward_stage(
        links, clip, first_tree, second_tree, length, norm, graph_one, skip_one, time_one_own, graph_two_own, time_two_own,
        (cotangent_own, cotangent_other),
    )
    spatial_two = spatial_two[0]
    block_received = exchange(block_other)
    old_moments = (by_group(first_graph_moment), first_time_moment, first_skip_moment[None], by_group(second_graph_moment), second_time_moment)
    flat = lambda tensor: tensor.reshape(-1, local)
    (
        keep, early_received, late_received, time_two_reduced, graph_two_reduced, time_one_reduced, small_reduced,
        product_time, product_graph, total6, total7, total8, edge_sums,
    ) = backward_stage(
        links, length, (up, temporal_two, spatial_two, middle, temporal, skipped, spatial, clip), (time_two, graph_two, time_one),
        (flat(old_moments[4]), flat(old_moments[3]), flat(old_moments[1])), (graph_one, skip_one),
        (flat(old_moments[2]), flat(old_moments[0])), norm, first_tree, second_tree, (total1, total2, total3, total4, total5),
    )
    order = (4, 3, 1, 2, 0)
    in_order = lambda tensors: [tensors[slot] for slot in order]
    moments, nexts, copies = [
        {slot: tensor for slot, tensor in zip(order, tensors)}
        for tensors in muon_update(
            (time_two_reduced, graph_two_reduced, time_one_reduced, small_reduced),
            (1, 1, 1, 2),
            in_order(old_moments),
            in_order(weights),
            (True, False, True, False, False),
            (product_time, product_graph),
        )
    ]
    input_grad = jnp.transpose(frames_out(keep, (early_received, late_received), frame_count), (0, 3, 1, 2))

    def as_given(tensors):
        return (by_group(tensors[0]), tensors[1], tensors[2][0], by_group(tensors[3]), tensors[4])

    def both_clips(own, received):
        return jnp.where(half_index == 0, jnp.stack([own, received]), jnp.stack([received, own]))

    block = both_clips(block_own, block_received).reshape(2, LO, joints, PAD, local)[:, :, :, :hi_count]
    block_out = jnp.transpose(block, (0, 3, 1, 2, 4)).reshape(2, half_count, joints, local)

    gain_rows = jnp.stack([total8[1], total7[1], total7[2], total6[1], total5[1]])
    bias_rows = jnp.stack([total8[0], total7[0], total7[0], total6[0], total5[0]])
    norm_grad = jnp.stack([gain_rows, bias_rows])[:, :, :local]
    norm_moment_next = plain_decay * norm_moment + norm_grad
    norm_param_next = norm_param - plain_rate * norm_moment_next
    edge_sums = edge_sums[:6, :joints].reshape(2, 3, joints)
    empty = jnp.zeros((1, joints, joints), f32)
    edge_dense = jnp.stack(
        [edge_sums[:, 0][:, None, :] + empty, edge_sums[:, 1][:, :, None] + empty, edge_sums[:, 2][:, None, :] + empty], axis=1
    )
    edge_grad = jnp.where(placed[None], edge_dense, 0.0) * inverse[None, None, None, :]
    edge_moment_next = plain_decay * edge_moment + edge_grad
    edge_weight_next = edge_weight - plain_rate * edge_moment_next
    return (
        (block_out, input_grad)
        + as_given(moments)
        + as_given(nexts)
        + as_given(copies)
        + (norm_moment_next, norm_param_next, edge_moment_next, edge_weight_next)
    )


def solution(mesh):
    channel = P(None, None, "mp")
    skip = P(None, "mp")
    batch = P("dp", None, None, "mp")
    weight_specs = (channel, channel, skip, channel, channel)
    in_specs = (batch, P("dp"), batch, P()) + weight_specs + weight_specs + (channel, channel, P(), P())
    out_specs = (batch, batch) + weight_specs + weight_specs + weight_specs + (channel, channel, P(), P())
    return jax.shard_map(
        functools.partial(per_device, Links(mesh)), mesh=mesh, in_specs=in_specs, out_specs=out_specs, check_vma=False
    )
```
